512 devices in a mesh: pairs: 64 (over y, z), days: 8 (over x, core).
Axes of the slice: x: 4, y: 4, z: 16, core: 2. Of those that a mesh axis runs over, the one named last changes fastest.
Arguments:
- spectra: bfloat16 [2, 64, 96, 30, 8, 256], P(None, 'pairs', 'days'), may hold values from -5 to 5
- held_block: int32 [64], replicated, may hold values from 0 to 63, as said below
- partner: int32 [64], replicated, may hold values from 0 to 63, as said below
Outputs:
- stacked: float32 [64, 8, 2, 256, 256], P('pairs', 'days')
The draws below stay inside these ranges and needn't reach their ends.
Inputs may be any that keep to these rules, and one draw needn't show every extreme that they name: held_block is a permutation of the block numbers. partner[p] is the block held by device p - 1 or by device p + 1; devices 0 and 1 take each other, and so do devices 64 - 2 and 63.
All inputs are finite; a program needn't handle non-finite values.
Results may differ from the reference program's by a relative error of at most 0.0003.
Values may be sent and summed in bfloat16 or wider, within the bound.
A program may use at most 64 MiB of HBM per device.

```python
import math
import jax
import jax.numpy as jnp
from jax import lax

CH = 256
SEG = 30
BINS = 8
DAYS = 96
BLOCKS = 64


def tile_layout(key):
    swap_key, side_key = jax.random.split(key)
    numbers = jnp.arange(BLOCKS, dtype=jnp.int32)
    swapped = jax.random.randint(swap_key, (BLOCKS // 2,), 0, 2, dtype=jnp.int32)
    within = numbers % 2
    flipped = jnp.where(swapped[numbers // 2] == 1, 1 - within, within)
    held_blocks = numbers - within + flipped
    side_signs = jax.random.randint(side_key, (BLOCKS,), 0, 2, dtype=jnp.int32) * 2 - 1
    side_signs = jnp.where(numbers == 0, 1, jnp.where(numbers == BLOCKS - 1, -1, side_signs))
    side_signs = jnp.where(numbers == 1, -1, jnp.where(numbers == BLOCKS - 2, 1, side_signs))
    holders = numbers + side_signs
    return (held_blocks, held_blocks[holders])


def draw_held_block(key, part):
    return tile_layout(key)[0]


def draw_partner(key, part):
    return tile_layout(key)[1]


def shard_levels(own_key, shape, cuts, smallest, high):
    gain, own = 1.0, jax.random.fold_in(own_key, 6)
    for axis_at, parts in cuts:
        draws = jnp.exp(jax.random.uniform(jax.random.fold_in(own, axis_at), (parts,), jnp.float32, smallest / len(cuts), high / len(cuts)))
        gain = gain * jnp.repeat(draws, shape[axis_at] // parts).reshape([-1 if axis == axis_at else 1 for axis in range(len(shape))])
    return gain


def scatter_about(rng, dims, spread, most, cuts=(), held_as=jnp.bfloat16):
    entries = spread * jax.random.normal(rng, dims, jnp.float32)
    if cuts:
        entries = entries * shard_levels(rng, dims, cuts, -0.22, 0.18)
    return jnp.clip(entries, -most, most).astype(held_as)


def setup_inputs(seed: int = 0) -> dict:
    splits = jax.random.split(jax.random.key(seed), 4)
    spectra = scatter_about(splits[0], (2, BLOCKS, DAYS, SEG, BINS, CH), 0.7, 5.0, ((1, 64), (2, 8)))
    held_block = draw_held_block(jax.random.fold_in(splits[3], 71), 0)
    partner = draw_partner(jax.random.fold_in(splits[3], 71), 0)
    return {"spectra": spectra, "held_block": held_block, "partner": partner}


def reference(spectra, held_block, partner):
    weighting = 1.0 / math.sqrt(DAYS * SEG)
    positions = jnp.arange(BLOCKS, dtype=jnp.int32)

    def one_tile(position):
        wanted = jnp.sum(jnp.where(positions == position, partner, 0)).astype(jnp.int32)
        holder = jnp.sum(jnp.where(held_block == wanted, positions, 0)).astype(jnp.int32)
        own_rows = lax.dynamic_index_in_dim(spectra, position, 1, keepdims=False).astype(jnp.float32)
        far_rows = lax.dynamic_index_in_dim(spectra, holder, 1, keepdims=False).astype(jnp.float32)
        own_rows = own_rows.reshape(2, DAYS * SEG, BINS, CH)
        far_rows = far_rows.reshape(2, DAYS * SEG, BINS, CH)
        real_part = jnp.einsum('tfa,tfb->fab', own_rows[0], far_rows[0]) + jnp.einsum('tfa,tfb->fab', own_rows[1], far_rows[1])
        imag_part = jnp.einsum('tfa,tfb->fab', own_rows[1], far_rows[0]) - jnp.einsum('tfa,tfb->fab', own_rows[0], far_rows[1])
        return jnp.stack([real_part, imag_part], 1) * weighting
    return lax.map(one_tile, positions)
```

```python
import functools
import math

import jax
import jax.numpy as jnp
from jax import lax
from jax.experimental import pallas as pl
from jax.experimental.pallas import tpu as pltpu
from jax.sharding import PartitionSpec as P

MESH = pl.DeviceIdType.MESH
LANES = 128
GROUP = 8
STEP = 24


def kernel(
    n_pairs, n_x, weight, held_ref, partner_ref, x_ref, out_ref,
    x_in, stage, grid_own, to_core, far, wide, tiles, parts, back, view,
    in_sem, core_send, core_recv, z_send, z_recv, part_send, part_recv, back_send, back_recv,
):
    n_time = x_in.shape[1]
    n_tiles = 2 * n_x
    p = lax.axis_index("pairs")
    d = lax.axis_index("days")
    x = d // 2
    core = d % 2
    up = 1 - 2 * core
    z_to = (p + up + n_pairs) % n_pairs
    z_from = (p - up + n_pairs) % n_pairs
    other = d + 1 - 2 * core

    barrier = pltpu.get_barrier_semaphore()
    peers = [(p, other), (z_to, d), (z_from, d)]
    peers += [(p, (x + k) % n_x * 2 + core) for k in range(1, n_x)]
    for peer in peers:
        pl.semaphore_signal(barrier, inc=1, device_id=peer, device_id_type=MESH)

    chunks = in_sem.shape[0]
    rows = n_time // chunks
    loads = [
        pltpu.make_async_copy(
            x_ref.at[:, pl.ds(k * rows, rows)], x_in.at[:, pl.ds(k * rows, rows)], in_sem.at[k]
        )
        for k in range(chunks)
    ]
    for load in loads:
        load.start()

    bins = 2 * n_x

    def relayout(i, carry):
        t0 = pl.multiple_of(i * STEP, GROUP)
        for part in range(2):
            block = x_in[part, pl.ds(t0, STEP)].astype(jnp.float32).reshape(STEP * bins, 2 * LANES)
            stage[part, 0] = block[:, :LANES]
            stage[part, 1] = block[:, LANES:]
        r0 = pl.multiple_of(i * 2 * STEP, 16)
        for f in range(bins):
            for half in range(2):
                both = [
                    stage[part, half, pl.ds(f, STEP, stride=bins), :].reshape(STEP // GROUP, 1, GROUP, LANES)
                    for part in range(2)
                ]
                block = jnp.concatenate(both, axis=1).reshape(2 * STEP, LANES).astype(jnp.bfloat16)
                where = (f + core) % 2 * n_x + f // 2
                grid_own[where, half, pl.ds(r0, 2 * STEP), :] = block
        return carry

    for k in range(chunks):
        loads[k].wait()
        lax.fori_loop(k * (rows // STEP), (k + 1) * (rows // STEP), relayout, 0)

    pl.semaphore_wait(barrier, len(peers))

    def owner(i):
        return (x + 1 + i) % n_x

    def core_copy(i):
        return pltpu.make_async_remote_copy(
            src_ref=grid_own.at[n_x + owner(i)],
            dst_ref=to_core.at[owner(i)],
            send_sem=core_send.at[i],
            recv_sem=core_recv.at[i],
            device_id=(p, other),
            device_id_type=MESH,
        )

    def z_copy(q, source):
        held = grid_own if source == 0 else to_core
        return pltpu.make_async_remote_copy(
            src_ref=held.at[owner(q // 2), q % 2],
            dst_ref=far.at[q, source],
            send_sem=z_send.at[q, source],
            recv_sem=z_recv.at[q, source],
            device_id=(z_to, d),
            device_id_type=MESH,
        )

    def part_copy(q):
        return pltpu.make_async_remote_copy(
            src_ref=tiles.at[q],
            dst_ref=parts.at[q],
            send_sem=part_send.at[q],
            recv_sem=part_recv.at[q],
            device_id=(p, owner(q // 2) * 2 + core),
            device_id_type=MESH,
        )

    def back_copy(half):
        return pltpu.make_async_remote_copy(
            src_ref=tiles.at[n_tiles - 2 + half],
            dst_ref=back.at[half],
            send_sem=back_send.at[half],
            recv_sem=back_recv.at[half],
            device_id=(z_from, d),
            device_id_type=MESH,
        )

    z_copy(0, 0).start()
    for i in range(n_x):
        core_copy(i).start()
    core_copy(0).wait_recv()
    z_copy(0, 1).start()

    def one_tile(q, carry):
        i, half = q // 2, q % 2

        @pl.when((half == 1) & (i < n_x - 1))
        def _():
            core_copy(i + 1).wait_recv()

        @pl.when(q < n_tiles - 1)
        def _():
            z_copy(q + 1, 0).start()
            z_copy(q + 1, 1).start()

        for source, held in enumerate((grid_own, to_core)):
            for side in range(2):
                own = held[owner(i), side]
                wide[:, pl.ds(side * LANES, LANES)] = own
                own = own.astype(jnp.float32).reshape(-1, 2, GROUP, LANES)
                turned = jnp.concatenate([-own[:, 1:], own[:, :1]], axis=1)
                wide[:, pl.ds((2 + side) * LANES, LANES)] = turned.reshape(-1, LANES).astype(jnp.bfloat16)
            z_copy(q, source).wait_recv()
            product = lax.dot_general(
                far[q, source], wide[...], (((0,), (0,)), ((), ())), preferred_element_type=jnp.float32
            )
            if source == 0:
                tiles[q] = product
            else:
                tiles[q] += product

        @pl.when(i < n_x - 1)
        def _():
            part_copy(q).start()

        @pl.when(i == n_x - 1)
        def _():
            for k in range(n_x - 1):
                part_copy(2 * k + half).wait_recv()
                tiles[q] += parts[2 * k + half]
            back_copy(half).start()

        return carry

    lax.fori_loop(0, n_tiles, one_tile, 0)

    for half in range(2):
        tile = tiles[n_tiles - 2 + half]
        view[0, :, pl.ds(half * LANES, LANES)] = tile[:, : 2 * LANES].T
        view[1, :, pl.ds(half * LANES, LANES)] = -tile[:, 2 * LANES :].T
    mine = held_ref[z_from] == partner_ref[p]
    for half in range(2):
        back_copy(half).wait_recv()
        spot = pl.ds(half * LANES, LANES)
        for part in range(2):
            sent = back[half, :, pl.ds(part * 2 * LANES, 2 * LANES)]
            out_ref[part, spot, :] = jnp.where(mine, view[part, spot, :], sent) * weight

    for i in range(n_x):
        core_copy(i).wait_send()
    for q in range(n_tiles):
        z_copy(q, 0).wait_send()
        z_copy(q, 1).wait_send()
    for q in range(n_tiles - 2):
        part_copy(q).wait_send()
    for half in range(2):
        back_copy(half).wait_send()


def per_device(spectra, held_block, partner):
    n_pairs, n_days = lax.axis_size("pairs"), lax.axis_size("days")
    _, _, days, segments, bins, channels = spectra.shape
    n_time = days * segments
    n_x, n_tiles = n_days // 2, n_days
    block = 2 * n_time
    weight = 1.0 / math.sqrt(n_days * n_time)
    dma = pltpu.SemaphoreType.DMA
    out = pl.pallas_call(
        functools.partial(kernel, n_pairs, n_x, weight),
        out_shape=jax.ShapeDtypeStruct((2, channels, channels), jnp.float32),
        in_specs=[
            pl.BlockSpec(memory_space=pltpu.SMEM),
            pl.BlockSpec(memory_space=pltpu.SMEM),
            pl.BlockSpec(memory_space=pl.ANY),
        ],
        out_specs=pl.BlockSpec(memory_space=pltpu.VMEM),
        scratch_shapes=[
            pltpu.VMEM((2, n_time, bins, channels), jnp.bfloat16),
            pltpu.VMEM((2, 2, STEP * bins, LANES), jnp.float32),
            pltpu.VMEM((bins, 2, block, LANES), jnp.bfloat16),
            pltpu.VMEM((n_x, 2, block, LANES), jnp.bfloat16),
            pltpu.VMEM((n_tiles, 2, block, LANES), jnp.bfloat16),
            pltpu.VMEM((block, 4 * LANES), jnp.bfloat16),
            pltpu.VMEM((n_tiles, LANES, 4 * LANES), jnp.float32),
            pltpu.VMEM((n_tiles - 2, LANES, 4 * LANES), jnp.float32),
            pltpu.VMEM((2, LANES, 4 * LANES), jnp.float32),
            pltpu.VMEM((2, channels, channels), jnp.float32),
            dma((3,)),
            dma((n_x,)),
            dma((n_x,)),
            dma((n_tiles, 2)),
            dma((n_tiles, 2)),
            dma((n_tiles - 2,)),
            dma((n_tiles - 2,)),
            dma((2,)),
            dma((2,)),
        ],
        compiler_params=pltpu.CompilerParams(
            collective_id=0, has_side_effects=True, vmem_limit_bytes=48 * 1024 * 1024
        ),
        cost_estimate=pl.CostEstimate(flops=8 * bins * n_time * channels**2, bytes_accessed=4 * block * bins * channels, transcendentals=0),
    )(held_block, partner, spectra.reshape(2, n_time, bins, channels))
    return out[None, None]


def solution(mesh):
    in_specs = (P(None, "pairs", "days", None, None, None), P(), P())
    out_specs = P("pairs", "days", None, None, None)
    return jax.shard_map(
        per_device, mesh=mesh, in_specs=in_specs, out_specs=out_specs, check_vma=False
    )
```

```python
import functools
import math

import jax
import jax.numpy as jnp
from jax import lax
from jax.experimental import pallas as pl
from jax.experimental.pallas import tpu as pltpu
from jax.sharding import PartitionSpec as P

MESH = pl.DeviceIdType.MESH
LANES = 128
GROUP = 8
STEP = 24


def kernel(
    n_pairs, n_x, weight, held_hbm, partner_hbm, x_ref, out_ref,
    held_ref, partner_ref,    x_in, stage, grid_own, to_core, far, wide, tiles, parts, back, view,
    in_sem, core_send, core_recv, z_send, z_recv, part_send, part_recv, back_send, back_recv,
):
    n_time = x_in.shape[1]
    n_tiles = 2 * n_x
    p = lax.axis_index("pairs")
    d = lax.axis_index("days")
    x = d // 2
    core = d % 2
    up = 1 - 2 * core
    z_to = (p + up + n_pairs) % n_pairs
    z_from = (p - up + n_pairs) % n_pairs
    other = d + 1 - 2 * core
    last = (n_pairs - 1) * core
    has_from = p != last
    has_to = p != n_pairs - 1 - last

    barrier = pltpu.get_barrier_semaphore()
    peers = [(p, other)] + [(p, (x + k) % n_x * 2 + core) for k in range(1, n_x)]
    for peer in peers:
        pl.semaphore_signal(barrier, inc=1, device_id=peer, device_id_type=MESH)

    @pl.when(has_from)
    def _():
        pl.semaphore_signal(barrier, inc=1, device_id=(z_from, d), device_id_type=MESH)

    chunks = in_sem.shape[0] - 2
    rows = n_time // chunks
    loads = [
        pltpu.make_async_copy(
            x_ref.at[:, pl.ds(k * rows, rows)], x_in.at[:, pl.ds(k * rows, rows)], in_sem.at[k]
        )
        for k in range(chunks)
    ]
    orders = [
        pltpu.make_async_copy(held_hbm, held_ref, in_sem.at[chunks]),
        pltpu.make_async_copy(partner_hbm, partner_ref, in_sem.at[chunks + 1]),
    ]
    for load in loads + orders:
        load.start()

    bins = 2 * n_x

    def relayout(i, carry):
        t0 = pl.multiple_of(i * STEP, GROUP)
        for part in range(2):
            block = x_in[part, pl.ds(t0, STEP)].astype(jnp.float32).reshape(STEP * bins, 2 * LANES)
            stage[part, 0] = block[:, :LANES]
            stage[part, 1] = block[:, LANES:]
        r0 = pl.multiple_of(i * 2 * STEP, 16)
        for f in range(bins):
            for half in range(2):
                both = [
                    stage[part, half, pl.ds(f, STEP, stride=bins), :].reshape(STEP // GROUP, 1, GROUP, LANES)
                    for part in range(2)
                ]
                block = jnp.concatenate(both, axis=1).reshape(2 * STEP, LANES).astype(jnp.bfloat16)
                where = (f + core) % 2 * n_x + f // 2
                grid_own[where, half, pl.ds(r0, 2 * STEP), :] = block
        return carry

    for k in range(chunks):
        loads[k].wait()
        lax.fori_loop(k * (rows // STEP), (k + 1) * (rows // STEP), relayout, 0)

    pl.semaphore_wait(barrier, len(peers) + has_to.astype(jnp.int32))

    def owner(i):
        return (x + 1 + i) % n_x

    def core_copy(i):
        return pltpu.make_async_remote_copy(
            src_ref=grid_own.at[n_x + owner(i)],
            dst_ref=to_core.at[owner(i)],
            send_sem=core_send.at[i],
            recv_sem=core_recv.at[i],
            device_id=(p, other),
            device_id_type=MESH,
        )

    def z_copy(q, source):
        held = grid_own if source == 0 else to_core
        return pltpu.make_async_remote_copy(
            src_ref=held.at[owner(q // 2), q % 2],
            dst_ref=far.at[q, source],
            send_sem=z_send.at[q, source],
            recv_sem=z_recv.at[q, source],
            device_id=(z_to, d),
            device_id_type=MESH,
        )

    def part_copy(q):
        return pltpu.make_async_remote_copy(
            src_ref=tiles.at[q],
            dst_ref=parts.at[q],
            send_sem=part_send.at[q],
            recv_sem=part_recv.at[q],
            device_id=(p, owner(q // 2) * 2 + core),
            device_id_type=MESH,
        )

    def back_copy(half):
        return pltpu.make_async_remote_copy(
            src_ref=tiles.at[n_tiles - 2 + half],
            dst_ref=back.at[half],
            send_sem=back_send.at[half],
            recv_sem=back_recv.at[half],
            device_id=(z_from, d),
            device_id_type=MESH,
        )

    @pl.when(has_to)
    def _():
        z_copy(0, 0).start()

    for i in range(n_x):
        core_copy(i).start()
    for i in range(n_x):
        core_copy(i).wait_recv()

        @pl.when(has_to)
        def _():
            if i > 0:
                z_copy(2 * i, 0).start()
            z_copy(2 * i, 1).start()
            z_copy(2 * i + 1, 0).start()
            z_copy(2 * i + 1, 1).start()

    def one_tile(q, carry):
        i, half = q // 2, q % 2

        for source, held in enumerate((grid_own, to_core)):
            for side in range(2):
                own = held[owner(i), side]
                wide[:, pl.ds(side * LANES, LANES)] = own
                own = own.astype(jnp.float32).reshape(-1, 2, GROUP, LANES)
                turned = jnp.concatenate([-own[:, 1:], own[:, :1]], axis=1)
                wide[:, pl.ds((2 + side) * LANES, LANES)] = turned.reshape(-1, LANES).astype(jnp.bfloat16)
            z_copy(q, source).wait_recv()
            product = lax.dot_general(
                far[q, source], wide[...], (((0,), (0,)), ((), ())), preferred_element_type=jnp.float32
            )
            if source == 0:
                tiles[q] = product
            else:
                tiles[q] += product

        @pl.when(i < n_x - 1)
        def _():
            part_copy(q).start()

        @pl.when(i == n_x - 1)
        def _():
            for k in range(n_x - 1):
                part_copy(2 * k + half).wait_recv()
                tiles[q] += parts[2 * k + half]
            back_copy(half).start()

        return carry

    @pl.when(has_from)
    def _():
        lax.fori_loop(0, n_tiles, one_tile, 0)
        for half in range(2):
            tile = tiles[n_tiles - 2 + half]
            view[0, :, pl.ds(half * LANES, LANES)] = tile[:, : 2 * LANES].T
            view[1, :, pl.ds(half * LANES, LANES)] = -tile[:, 2 * LANES :].T

    @pl.when(jnp.logical_not(has_from))
    def _():
        view[...] = jnp.zeros_like(view)

    @pl.when(jnp.logical_not(has_to))
    def _():
        back[...] = jnp.zeros_like(back)

    for order in orders:
        order.wait()
    mine = held_ref[z_from] == partner_ref[p]
    for half in range(2):

        @pl.when(has_to)
        def _():
            back_copy(half).wait_recv()

        spot = pl.ds(half * LANES, LANES)
        for part in range(2):
            sent = back[half, :, pl.ds(part * 2 * LANES, 2 * LANES)]
            out_ref[part, spot, :] = jnp.where(mine, view[part, spot, :], sent) * weight

    for i in range(n_x):
        core_copy(i).wait_send()

    @pl.when(has_to)
    def _():
        for q in range(n_tiles):
            z_copy(q, 0).wait_send()
            z_copy(q, 1).wait_send()

    @pl.when(has_from)
    def _():
        for q in range(n_tiles - 2):
            part_copy(q).wait_send()
        for half in range(2):
            back_copy(half).wait_send()


def per_device(spectra, held_block, partner):
    n_pairs, n_days = lax.axis_size("pairs"), lax.axis_size("days")
    _, _, days, segments, bins, channels = spectra.shape
    n_time = days * segments
    n_x, n_tiles = n_days // 2, n_days
    block = 2 * n_time
    weight = 1.0 / math.sqrt(n_days * n_time)
    dma = pltpu.SemaphoreType.DMA
    out = pl.pallas_call(
        functools.partial(kernel, n_pairs, n_x, weight),
        out_shape=jax.ShapeDtypeStruct((2, channels, channels), jnp.float32),
        in_specs=[
            pl.BlockSpec(memory_space=pltpu.HBM),
            pl.BlockSpec(memory_space=pltpu.HBM),
            pl.BlockSpec(memory_space=pltpu.HBM),
        ],
        out_specs=pl.BlockSpec(memory_space=pltpu.VMEM),
        scratch_shapes=[
            pltpu.SMEM((n_pairs,), jnp.int32),
            pltpu.SMEM((n_pairs,), jnp.int32),
            pltpu.VMEM((2, n_time, bins, channels), jnp.bfloat16),
            pltpu.VMEM((2, 2, STEP * bins, LANES), jnp.float32),
            pltpu.VMEM((bins, 2, block, LANES), jnp.bfloat16),
            pltpu.VMEM((n_x, 2, block, LANES), jnp.bfloat16),
            pltpu.VMEM((n_tiles, 2, block, LANES), jnp.bfloat16),
            pltpu.VMEM((block, 4 * LANES), jnp.bfloat16),
            pltpu.VMEM((n_tiles, LANES, 4 * LANES), jnp.float32),
            pltpu.VMEM((n_tiles - 2, LANES, 4 * LANES), jnp.float32),
            pltpu.VMEM((2, LANES, 4 * LANES), jnp.float32),
            pltpu.VMEM((2, channels, channels), jnp.float32),
            dma((5,)),
            dma((n_x,)),
            dma((n_x,)),
            dma((n_tiles, 2)),
            dma((n_tiles, 2)),
            dma((n_tiles - 2,)),
            dma((n_tiles - 2,)),
            dma((2,)),
            dma((2,)),
        ],
        compiler_params=pltpu.CompilerParams(
            collective_id=0, has_side_effects=True, vmem_limit_bytes=62 * 1024 * 1024
        ),
        cost_estimate=pl.CostEstimate(flops=8 * bins * n_time * channels**2, bytes_accessed=4 * block * bins * channels, transcendentals=0),
    )(held_block, partner, spectra.reshape(2, n_time, bins, channels))
    return out[None, None]


def solution(mesh):
    in_specs = (P(None, "pairs", "days", None, None, None), P(), P())
    out_specs = P("pairs", "days", None, None, None)
    return jax.shard_map(
        per_device, mesh=mesh, in_specs=in_specs, out_specs=out_specs, check_vma=False
    )
```

```python
import functools
import math

import jax
import jax.numpy as jnp
from jax import lax
from jax.experimental import pallas as pl
from jax.experimental.pallas import tpu as pltpu
from jax.sharding import PartitionSpec as P

MESH = pl.DeviceIdType.MESH
LANES = 128
GROUP = 8
LEVELS = 32767.0
TINY = 2e-34
STEP = 24


def kernel(
    n_pairs, n_x, weight, held_hbm, partner_hbm, x_ref, out_ref,
    held_ref, partner_ref,    x_in, stage, grid_own, to_core, far, wide, tiles, parts, sent, sent_top, back, back_top, view,
    in_sem, core_send, core_recv, z_send, z_recv, part_send, part_recv, back_send, back_recv,
):
    n_time = x_in.shape[1]
    n_tiles = 2 * n_x
    p = lax.axis_index("pairs")
    d = lax.axis_index("days")
    x = d // 2
    core = d % 2
    up = 1 - 2 * core
    z_to = (p + up + n_pairs) % n_pairs
    z_from = (p - up + n_pairs) % n_pairs
    other = d + 1 - 2 * core
    last = (n_pairs - 1) * core
    has_from = p != last
    has_to = p != n_pairs - 1 - last

    barrier = pltpu.get_barrier_semaphore()
    peers = [(p, other)] + [(p, (x + k) % n_x * 2 + core) for k in range(1, n_x)]
    for peer in peers:
        pl.semaphore_signal(barrier, inc=1, device_id=peer, device_id_type=MESH)

    @pl.when(has_from)
    def _():
        pl.semaphore_signal(barrier, inc=1, device_id=(z_from, d), device_id_type=MESH)

    chunks = in_sem.shape[0] - 2
    rows = n_time // chunks
    loads = [
        pltpu.make_async_copy(
            x_ref.at[:, pl.ds(k * rows, rows)], x_in.at[:, pl.ds(k * rows, rows)], in_sem.at[k]
        )
        for k in range(chunks)
    ]
    orders = [
        pltpu.make_async_copy(held_hbm, held_ref, in_sem.at[chunks]),
        pltpu.make_async_copy(partner_hbm, partner_ref, in_sem.at[chunks + 1]),
    ]
    for load in loads + orders:
        load.start()

    bins = 2 * n_x

    def owner(i):
        return (x + up * (1 + i) + n_x) % n_x


    def relayout(i, carry):
        t0 = pl.multiple_of(i * STEP, GROUP)
        for part in range(2):
            block = x_in[part, pl.ds(t0, STEP)].astype(jnp.float32).reshape(STEP * bins, 2 * LANES)
            stage[part, 0] = block[:, :LANES]
            stage[part, 1] = block[:, LANES:]
        r0 = pl.multiple_of(i * 2 * STEP, 16)
        for f in range(bins):
            for half in range(2):
                both = [
                    stage[part, half, pl.ds(f, STEP, stride=bins), :].reshape(STEP // GROUP, 1, GROUP, LANES)
                    for part in range(2)
                ]
                block = jnp.concatenate(both, axis=1).reshape(2 * STEP, LANES).astype(jnp.bfloat16)
                where = (f + core) % 2 * n_x + f // 2
                grid_own[where, half, pl.ds(r0, 2 * STEP), :] = block
        return carry

    def core_copy(i):
        theirs = (x - up * (1 + i) + n_x) % n_x
        return pltpu.make_async_remote_copy(
            src_ref=grid_own.at[n_x + theirs],
            dst_ref=to_core.at[theirs],
            send_sem=core_send.at[i],
            recv_sem=core_recv.at[i],
            device_id=(p, other),
            device_id_type=MESH,
        )

    def z_copy(q, source):
        held = grid_own if source == 0 else to_core
        return pltpu.make_async_remote_copy(
            src_ref=held.at[owner(q // 2), q % 2],
            dst_ref=far.at[q, source],
            send_sem=z_send.at[q, source],
            recv_sem=z_recv.at[q, source],
            device_id=(z_to, d),
            device_id_type=MESH,
        )

    def part_copy(q):
        return pltpu.make_async_remote_copy(
            src_ref=tiles.at[q],
            dst_ref=parts.at[q],
            send_sem=part_send.at[q],
            recv_sem=part_recv.at[q],
            device_id=(p, owner(q // 2) * 2 + core),
            device_id_type=MESH,
        )

    def back_copies(half):
        return [
            pltpu.make_async_remote_copy(
                src_ref=source.at[half],
                dst_ref=target.at[half],
                send_sem=back_send.at[half, k],
                recv_sem=back_recv.at[half, k],
                device_id=(z_from, d),
                device_id_type=MESH,
            )
            for k, (source, target) in enumerate(((sent_top, back_top), (sent, back)))
        ]

    for k in range(chunks):
        loads[k].wait()
        lax.fori_loop(k * (rows // STEP), (k + 1) * (rows // STEP), relayout, 0)
        if k == 0:
            pl.semaphore_wait(barrier, len(peers) + has_to.astype(jnp.int32))

        @pl.when(has_to)
        def _():
            for q in range(2):
                part = pl.ds(k * 2 * rows, 2 * rows)
                pltpu.make_async_remote_copy(
                    src_ref=grid_own.at[owner(0), q, part],
                    dst_ref=far.at[q, 0, part],
                    send_sem=z_send.at[q, 0],
                    recv_sem=z_recv.at[q, 0],
                    device_id=(z_to, d),
                    device_id_type=MESH,
                ).start()

    for i in range(n_x):
        core_copy(i).start()
    for i in range(n_x):
        core_copy(i).wait_recv()

        @pl.when(has_to)
        def _():
            if i > 0:
                z_copy(2 * i, 0).start()
            z_copy(2 * i, 1).start()
            if i > 0:
                z_copy(2 * i + 1, 0).start()
            z_copy(2 * i + 1, 1).start()

    def one_tile(q, carry):
        i, half = q // 2, q % 2

        for source, held in enumerate((grid_own, to_core)):
            for side in range(2):
                own = held[owner(i), side]
                wide[:, pl.ds(side * LANES, LANES)] = own
                own = own.astype(jnp.float32).reshape(-1, 2, GROUP, LANES)
                turned = jnp.concatenate([-own[:, 1:], own[:, :1]], axis=1)
                wide[:, pl.ds((2 + side) * LANES, LANES)] = turned.reshape(-1, LANES).astype(jnp.bfloat16)
            z_copy(q, source).wait_recv()
            product = lax.dot_general(
                far[q, source], wide[...], (((0,), (0,)), ((), ())), preferred_element_type=jnp.float32
            )
            if source == 0:
                tiles[q] = product
            else:
                tiles[q] += product

        @pl.when(i < n_x - 1)
        def _():
            part_copy(q).start()

        @pl.when(i == n_x - 1)
        def _():
            for k in range(n_x - 1):
                part_copy(2 * k + half).wait_recv()
                tiles[q] += parts[2 * k + half]
            tile = tiles[q]
            top = jnp.maximum(jnp.max(jnp.abs(tile), axis=0, keepdims=True), TINY)
            sent_top[half] = jnp.broadcast_to(top, sent_top.shape[1:])
            sent[half] = jnp.round(tile * (LEVELS / top)).astype(jnp.int32).astype(jnp.int16)
            for copy in back_copies(half):
                copy.start()

        return carry

    @pl.when(has_from)
    def _():
        lax.fori_loop(0, n_tiles, one_tile, 0)
        for half in range(2):
            tile = tiles[n_tiles - 2 + half]
            view[0, :, pl.ds(half * LANES, LANES)] = tile[:, : 2 * LANES].T
            view[1, :, pl.ds(half * LANES, LANES)] = -tile[:, 2 * LANES :].T

    @pl.when(jnp.logical_not(has_from))
    def _():
        view[...] = jnp.zeros_like(view)

    @pl.when(jnp.logical_not(has_to))
    def _():
        back[...] = jnp.zeros_like(back)
        back_top[...] = jnp.zeros_like(back_top)

    for order in orders:
        order.wait()
    mine = held_ref[z_from] == partner_ref[p]
    for half in range(2):

        @pl.when(has_to)
        def _():
            for copy in back_copies(half):
                copy.wait_recv()

        spot = pl.ds(half * LANES, LANES)
        for part in range(2):
            lanes = pl.ds(part * 2 * LANES, 2 * LANES)
            theirs = back[half, :, lanes].astype(jnp.int32).astype(jnp.float32) * (back_top[half, :1, lanes] / LEVELS)
            out_ref[part, spot, :] = jnp.where(mine, view[part, spot, :], theirs) * weight

    for i in range(n_x):
        core_copy(i).wait_send()

    @pl.when(has_to)
    def _():
        for q in range(n_tiles):
            z_copy(q, 0).wait_send()
            z_copy(q, 1).wait_send()

    @pl.when(has_from)
    def _():
        for q in range(n_tiles - 2):
            part_copy(q).wait_send()
        for half in range(2):
            for copy in back_copies(half):
                copy.wait_send()


def per_device(spectra, held_block, partner):
    n_pairs, n_days = lax.axis_size("pairs"), lax.axis_size("days")
    _, _, days, segments, bins, channels = spectra.shape
    n_time = days * segments
    n_x, n_tiles = n_days // 2, n_days
    block = 2 * n_time
    weight = 1.0 / math.sqrt(n_days * n_time)
    dma = pltpu.SemaphoreType.DMA
    operands = (held_block, partner, spectra.reshape(2, n_time, bins, channels))
    out = pl.pallas_call(
        functools.partial(kernel, n_pairs, n_x, weight),
        out_shape=jax.ShapeDtypeStruct((2, channels, channels), jnp.float32),
        in_specs=[
            pl.BlockSpec(memory_space=pltpu.HBM),
            pl.BlockSpec(memory_space=pltpu.HBM),
            pl.BlockSpec(memory_space=pltpu.HBM),
        ],
        out_specs=pl.BlockSpec(memory_space=pltpu.VMEM),
        scratch_shapes=[
            pltpu.SMEM((n_pairs,), jnp.int32),
            pltpu.SMEM((n_pairs,), jnp.int32),
            pltpu.VMEM((2, n_time, bins, channels), jnp.bfloat16),
            pltpu.VMEM((2, 2, STEP * bins, LANES), jnp.float32),
            pltpu.VMEM((bins, 2, block, LANES), jnp.bfloat16),
            pltpu.VMEM((n_x, 2, block, LANES), jnp.bfloat16),
            pltpu.VMEM((n_tiles, 2, block, LANES), jnp.bfloat16),
            pltpu.VMEM((block, 4 * LANES), jnp.bfloat16),
            pltpu.VMEM((n_tiles, LANES, 4 * LANES), jnp.float32),
            pltpu.VMEM((n_tiles - 2, LANES, 4 * LANES), jnp.float32),
            pltpu.VMEM((2, LANES, 4 * LANES), jnp.int16),
            pltpu.VMEM((2, GROUP, 4 * LANES), jnp.float32),
            pltpu.VMEM((2, LANES, 4 * LANES), jnp.int16),
            pltpu.VMEM((2, GROUP, 4 * LANES), jnp.float32),
            pltpu.VMEM((2, channels, channels), jnp.float32),
            dma((5,)),
            dma((n_x,)),
            dma((n_x,)),
            dma((n_tiles, 2)),
            dma((n_tiles, 2)),
            dma((n_tiles - 2,)),
            dma((n_tiles - 2,)),
            dma((2, 2)),
            dma((2, 2)),
        ],
        compiler_params=pltpu.CompilerParams(
            collective_id=0, has_side_effects=True, vmem_limit_bytes=48 * 1024 * 1024
        ),
        cost_estimate=pl.CostEstimate(flops=8 * bins * n_time * channels**2, bytes_accessed=4 * block * bins * channels, transcendentals=0),
    )(*(pltpu.with_memory_space_constraint(a, pltpu.HBM) for a in operands))
    return out[None, None]


def solution(mesh):
    in_specs = (P(None, "pairs", "days", None, None, None), P(), P())
    out_specs = P("pairs", "days", None, None, None)
    return jax.shard_map(
        per_device, mesh=mesh, in_specs=in_specs, out_specs=out_specs, check_vma=False
    )
```

```python
import functools
import math

import jax
import jax.numpy as jnp
from jax import lax
from jax.experimental import pallas as pl
from jax.experimental.pallas import tpu as pltpu
from jax.sharding import PartitionSpec as P

MESH = pl.DeviceIdType.MESH
LANES = 128
GROUP = 8
LEVELS = 32767.0
TINY = 2e-34
STEP = 24


def kernel(
    n_pairs, n_x, weight, held_hbm, partner_hbm, x_ref, out_ref,
    held_ref, partner_ref, x_in, stage, grid_own, to_core, far, wide, tiles, parts,
    sent, sent_top, back, back_top, view,
    in_sem, core_send, core_recv, z_send, z_recv, part_send, part_recv, back_send, back_recv,
):
    n_time = x_in.shape[1]
    n_tiles = 2 * n_x
    p = lax.axis_index("pairs")
    d = lax.axis_index("days")
    x = d // 2
    core = d % 2
    up = 1 - 2 * core
    z_to = (p + up + n_pairs) % n_pairs
    z_from = (p - up + n_pairs) % n_pairs
    other = d + 1 - 2 * core
    last = (n_pairs - 1) * core
    has_from = p != last
    has_to = p != n_pairs - 1 - last

    barrier = pltpu.get_barrier_semaphore()

    @pl.when(has_from)
    def _():
        pl.semaphore_signal(barrier, inc=1, device_id=(z_from, d), device_id_type=MESH)

    peers = [(p, other)] + [(p, (x + k) % n_x * 2 + core) for k in range(1, n_x)]
    for peer in peers:
        pl.semaphore_signal(barrier, inc=1, device_id=peer, device_id_type=MESH)

    chunks = in_sem.shape[0] - 2
    rows = n_time // chunks
    loads = [
        pltpu.make_async_copy(
            x_ref.at[:, pl.ds(k * rows, rows)], x_in.at[:, pl.ds(k * rows, rows)], in_sem.at[k]
        )
        for k in range(chunks)
    ]
    orders = [
        pltpu.make_async_copy(held_hbm, held_ref, in_sem.at[chunks]),
        pltpu.make_async_copy(partner_hbm, partner_ref, in_sem.at[chunks + 1]),
    ]
    for load in loads:
        load.start()

    bins = 2 * n_x

    def owner(i):
        return (x + up * (1 + i) + n_x) % n_x

    def relayout(i, carry):
        t0 = pl.multiple_of(i * STEP, GROUP)
        for part in range(2):
            block = x_in[part, pl.ds(t0, STEP)].astype(jnp.float32).reshape(STEP * bins, 2 * LANES)
            stage[part, 0, pl.ds(0, STEP * bins), :] = block[:, :LANES]
            stage[part, 1, pl.ds(0, STEP * bins), :] = block[:, LANES:]
        r0 = pl.multiple_of(i * 2 * STEP, 16)
        for f in range(bins):
            for half in range(2):
                both = [
                    stage[part, half, pl.ds(f, STEP, stride=bins), :].reshape(STEP // GROUP, 1, GROUP, LANES)
                    for part in range(2)
                ]
                block = jnp.concatenate(both, axis=1).reshape(2 * STEP, LANES).astype(jnp.bfloat16)
                where = (f + core) % 2 * n_x + f // 2
                grid_own[where, half, pl.ds(r0, 2 * STEP), :] = block
        return carry

    def core_copy(i):
        theirs = (x - up * (1 + i) + n_x) % n_x
        return pltpu.make_async_remote_copy(
            src_ref=grid_own.at[n_x + theirs],
            dst_ref=to_core.at[theirs],
            send_sem=core_send.at[i],
            recv_sem=core_recv.at[i],
            device_id=(p, other),
            device_id_type=MESH,
        )

    def z_copy(q, source):
        held = grid_own if source == 0 else to_core
        return pltpu.make_async_remote_copy(
            src_ref=held.at[owner(q // 2), q % 2],
            dst_ref=far.at[q, source],
            send_sem=z_send.at[q, source],
            recv_sem=z_recv.at[q, source],
            device_id=(z_to, d),
            device_id_type=MESH,
        )

    def part_copy(q):
        return pltpu.make_async_remote_copy(
            src_ref=tiles.at[q],
            dst_ref=parts.at[q],
            send_sem=part_send.at[q],
            recv_sem=part_recv.at[q],
            device_id=(p, owner(q // 2) * 2 + core),
            device_id_type=MESH,
        )

    def back_copies(half):
        return [
            pltpu.make_async_remote_copy(
                src_ref=source.at[half],
                dst_ref=target.at[half],
                send_sem=back_send.at[half, k],
                recv_sem=back_recv.at[half, k],
                device_id=(z_from, d),
                device_id_type=MESH,
            )
            for k, (source, target) in enumerate(((sent_top, back_top), (sent, back)))
        ]

    for k in range(chunks):
        loads[k].wait()
        lax.fori_loop(k * (rows // STEP), (k + 1) * (rows // STEP), relayout, 0)
        if k == 0:
            pl.semaphore_wait(barrier, len(peers) + has_to.astype(jnp.int32))

        @pl.when(has_to)
        def _():
            for q in range(2):
                part = pl.ds(k * 2 * rows, 2 * rows)
                pltpu.make_async_remote_copy(
                    src_ref=grid_own.at[owner(0), q, part],
                    dst_ref=far.at[q, 0, part],
                    send_sem=z_send.at[q, 0],
                    recv_sem=z_recv.at[q, 0],
                    device_id=(z_to, d),
                    device_id_type=MESH,
                ).start()

    for order in orders:
        order.start()
    for i in range(n_x):
        core_copy(i).start()
    for i in range(n_x):
        core_copy(i).wait_recv()

        @pl.when(has_to)
        def _():
            if i > 0:
                z_copy(2 * i, 0).start()
            z_copy(2 * i, 1).start()
            if i > 0:
                z_copy(2 * i + 1, 0).start()
            z_copy(2 * i + 1, 1).start()

    def one_tile(q, carry):
        i, half = q // 2, q % 2

        for source, held in enumerate((grid_own, to_core)):
            for side in range(2):
                own = held[owner(i), side]
                wide[:, pl.ds(side * LANES, LANES)] = own
                own = own.astype(jnp.float32).reshape(-1, 2, GROUP, LANES)
                turned = jnp.concatenate([-own[:, 1:], own[:, :1]], axis=1)
                wide[:, pl.ds((2 + side) * LANES, LANES)] = turned.reshape(-1, LANES).astype(jnp.bfloat16)
            z_copy(q, source).wait_recv()
            product = lax.dot_general(
                far[q, source], wide[...], (((0,), (0,)), ((), ())), preferred_element_type=jnp.float32
            )
            if source == 0:
                tiles[q] = product
            else:
                tiles[q] += product

        @pl.when(i < n_x - 1)
        def _():
            part_copy(q).start()

        @pl.when(i == n_x - 1)
        def _():
            for k in range(n_x - 1):
                part_copy(2 * k + half).wait_recv()
                tiles[q] += parts[2 * k + half]
            tile = tiles[q]
            top = jnp.maximum(jnp.max(jnp.abs(tile), axis=0, keepdims=True), TINY)
            sent_top[half] = jnp.broadcast_to(top, sent_top.shape[1:])
            back_copies(half)[0].start()
            sent[half] = jnp.round(tile * (LEVELS / top)).astype(jnp.int32).astype(jnp.int16)
            back_copies(half)[1].start()

        return carry

    @pl.when(has_from)
    def _():
        lax.fori_loop(0, n_tiles, one_tile, 0)
        for half in range(2):
            tile = tiles[n_tiles - 2 + half]
            view[0, :, pl.ds(half * LANES, LANES)] = tile[:, : 2 * LANES].T
            view[1, :, pl.ds(half * LANES, LANES)] = -tile[:, 2 * LANES :].T

    @pl.when(jnp.logical_not(has_from))
    def _():
        view[...] = jnp.zeros_like(view)

    @pl.when(jnp.logical_not(has_to))
    def _():
        back[...] = jnp.zeros_like(back)
        back_top[...] = jnp.zeros_like(back_top)

    for order in orders:
        order.wait()
    mine = held_ref[z_from] == partner_ref[p]
    for half in range(2):

        @pl.when(has_to)
        def _():
            for copy in back_copies(half):
                copy.wait_recv()

        spot = pl.ds(half * LANES, LANES)
        for part in range(2):
            lanes = pl.ds(part * 2 * LANES, 2 * LANES)
            theirs = back[half, :, lanes].astype(jnp.int32).astype(jnp.float32) * (back_top[half, :1, lanes] / LEVELS)
            out_ref[part, spot, :] = jnp.where(mine, view[part, spot, :], theirs) * weight

    for i in range(n_x):
        core_copy(i).wait_send()

    @pl.when(has_to)
    def _():
        for q in range(n_tiles):
            z_copy(q, 0).wait_send()
            z_copy(q, 1).wait_send()

    @pl.when(has_from)
    def _():
        for q in range(n_tiles - 2):
            part_copy(q).wait_send()
        for half in range(2):
            for copy in back_copies(half):
                copy.wait_send()


def per_device(spectra, held_block, partner):
    n_pairs, n_days = lax.axis_size("pairs"), lax.axis_size("days")
    _, _, days, segments, bins, channels = spectra.shape
    n_time = days * segments
    n_x, n_tiles = n_days // 2, n_days
    block = 2 * n_time
    weight = 1.0 / math.sqrt(n_days * n_time)
    dma = pltpu.SemaphoreType.DMA
    operands = (held_block, partner, spectra.reshape(2, n_time, bins, channels))
    out = pl.pallas_call(
        functools.partial(kernel, n_pairs, n_x, weight),
        out_shape=jax.ShapeDtypeStruct((2, channels, channels), jnp.float32),
        in_specs=[
            pl.BlockSpec(memory_space=pltpu.HBM),
            pl.BlockSpec(memory_space=pltpu.HBM),
            pl.BlockSpec(memory_space=pltpu.HBM),
        ],
        out_specs=pl.BlockSpec(memory_space=pltpu.VMEM),
        scratch_shapes=[
            pltpu.SMEM((n_pairs,), jnp.int32),
            pltpu.SMEM((n_pairs,), jnp.int32),
            pltpu.VMEM((2, n_time, bins, channels), jnp.bfloat16),
            pltpu.VMEM((2, 2, (STEP + 1) * bins, LANES), jnp.float32),
            pltpu.VMEM((bins, 2, block, LANES), jnp.bfloat16),
            pltpu.VMEM((n_x, 2, block, LANES), jnp.bfloat16),
            pltpu.VMEM((n_tiles, 2, block, LANES), jnp.bfloat16),
            pltpu.VMEM((block, 4 * LANES), jnp.bfloat16),
            pltpu.VMEM((n_tiles, LANES, 4 * LANES), jnp.float32),
            pltpu.VMEM((n_tiles - 2, LANES, 4 * LANES), jnp.float32),
            pltpu.VMEM((2, LANES, 4 * LANES), jnp.int16),
            pltpu.VMEM((2, GROUP, 4 * LANES), jnp.float32),
            pltpu.VMEM((2, LANES, 4 * LANES), jnp.int16),
            pltpu.VMEM((2, GROUP, 4 * LANES), jnp.float32),
            pltpu.VMEM((2, channels, channels), jnp.float32),
            dma((7,)),
            dma((n_x,)),
            dma((n_x,)),
            dma((n_tiles, 2)),
            dma((n_tiles, 2)),
            dma((n_tiles - 2,)),
            dma((n_tiles - 2,)),
            dma((2, 2)),
            dma((2, 2)),
        ],
        compiler_params=pltpu.CompilerParams(
            collective_id=0, has_side_effects=True, vmem_limit_bytes=48 * 1024 * 1024
        ),
        cost_estimate=pl.CostEstimate(flops=8 * bins * n_time * channels**2, bytes_accessed=4 * block * bins * channels, transcendentals=0),
    )(*(pltpu.with_memory_space_constraint(a, pltpu.HBM) for a in operands))
    return out[None, None]


def solution(mesh):
    in_specs = (P(None, "pairs", "days", None, None, None), P(), P())
    out_specs = P("pairs", "days", None, None, None)
    return jax.shard_map(
        per_device, mesh=mesh, in_specs=in_specs, out_specs=out_specs, check_vma=False
    )
```
